256 devices in a mesh: dp: 4 (over x), seq: 64 (over y, z, core).
Axes of the slice: x: 4, y: 4, z: 8, core: 2. Of those that a mesh axis runs over, the one named last changes fastest.
Arguments:
- spatial_qkv: bfloat16 [3, 32768, 1536], P(None, ('dp', 'seq')), parts along dimension 1, may hold values from -6 to 6
- temporal_qkv: bfloat16 [3, 32768, 1536], P(None, ('dp', 'seq')), parts along dimension 1, may hold values from -6 to 6
- cross_query: bfloat16 [32768, 1536], P(('dp', 'seq')), parts along dimension 0, may hold values from -6 to 6
- caption_kv: bfloat16 [1280, 2, 1536], P(('dp', 'seq')), parts along dimension 0, may hold values from -6 to 6
- out_grad: bfloat16 [32768, 1536], P(('dp', 'seq')), parts along dimension 0, may hold values from -6 to 6
- live_tokens: int32 [4], P('dp'), parts along dimension 0, may hold values from 2048 to 8192, as said below
- caption_len: int32 [4], P('dp'), parts along dimension 0, may hold values from 80 to 320, as said below
Outputs:
- mixed: bfloat16 [32768, 1536], P(('dp', 'seq')), parts along dimension 0
- spatial_grads: bfloat16 [3, 32768, 1536], P(None, ('dp', 'seq')), parts along dimension 1
- temporal_grads: bfloat16 [3, 32768, 1536], P(None, ('dp', 'seq')), parts along dimension 1
- cross_query_grad: bfloat16 [32768, 1536], P(('dp', 'seq')), parts along dimension 0
- caption_grads: float32 [1280, 2, 1536], P(('dp', 'seq')), parts along dimension 0
The draws below stay inside these ranges and needn't reach their ends.
There are 4 independent parts, one for each index of `dp`. The reference program is written for one: setup_inputs(seed, part) draws one part's arguments, and reference() takes and returns one part's arrays. A program takes and returns all parts, laid end to end along the dimension named above; each array names one. Nothing has to cross between parts.
Inputs may be any that keep to these rules, and one draw needn't show every extreme that they name: Tokens from live_tokens on are padding. Caption rows from caption_len on are padding.
All inputs are finite; a program needn't handle non-finite values.
Results may differ from the reference program's by a relative error of at most 0.035.
Values may be sent and summed in bfloat16 or wider, within the bound.
No kernel may reach another device: no remote copies, remote signals or barrier semaphores. Data moves between devices by JAX's collectives and lax.ppermute only.
A program may use at most 128 MiB of HBM per device.

```python
import jax
import jax.numpy as jnp
from jax import lax

HEADS = 12
HDIM = 128
P_SIZE = 512
CAPMAX = 320
HW = 1536
TOKENS = 8192


def draw_spatial_qkv(key, part):
    key = jax.random.fold_in(key, 3)
    key_one = jax.random.fold_in(key, 0)
    full_shape = (3, TOKENS, HEADS * HDIM)
    return jnp.clip(jax.random.normal(key_one, full_shape, jnp.float32), -6.0, 6.0).astype(jnp.bfloat16)


def draw_temporal_qkv(key, part):
    key = jax.random.fold_in(key, 5)
    key_one = jax.random.fold_in(key, 0)
    full_shape = (3, TOKENS, HEADS * HDIM)
    return jnp.clip(jax.random.normal(key_one, full_shape, jnp.float32), -6.0, 6.0).astype(jnp.bfloat16)


def draw_cross_query(key, part):
    key = jax.random.fold_in(key, 7)
    full_shape = (TOKENS, HEADS * HDIM)
    return jnp.clip(jax.random.normal(key, full_shape, jnp.float32), -6.0, 6.0).astype(jnp.bfloat16)


def draw_caption_kv(key, part):
    key = jax.random.fold_in(key, 8)
    key_one = jax.random.fold_in(key, 0)
    full_shape = (CAPMAX, 2, HEADS * HDIM)
    return jnp.clip(jax.random.normal(key_one, full_shape, jnp.float32), -6.0, 6.0).astype(jnp.bfloat16)


def draw_live_tokens(key, part):
    key = jax.random.fold_in(key, 9)
    drawn = jax.random.randint(key, (1,), TOKENS // 4, TOKENS + 1)
    return jnp.where(part == 1, TOKENS, drawn).astype(jnp.int32)


def draw_caption_len(key, part):
    key = jax.random.fold_in(key, 10)
    drawn = jax.random.randint(key, (1,), CAPMAX // 4, CAPMAX + 1)
    return jnp.where(part == 1, CAPMAX, drawn).astype(jnp.int32)


def block_scale(own_key, dims, cuts, smallest, high):
    level, own = 1.0, jax.random.fold_in(own_key, 6)
    for dim, shards_of in cuts:
        steps = jnp.exp(jax.random.uniform(jax.random.fold_in(own, dim), (shards_of,), jnp.float32, smallest / len(cuts), high / len(cuts)))
        level = level * jnp.repeat(steps, dims[dim] // shards_of).reshape([-1 if axis == dim else 1 for axis in range(len(dims))])
    return level


def scatter_about(key, extent, width, reach, cuts=(), kind=jnp.bfloat16):
    values = jax.random.normal(key, extent, jnp.float32) * width
    if len(cuts) > 0:
        values = block_scale(key, extent, cuts, -0.22, 0.18) * values
    return jnp.clip(values, min=-reach, max=reach).astype(kind)


def setup_inputs(seed: int = 0, part: int = 0) -> dict:
    seeds = jax.random.split(jax.random.key(seed), 8)
    part_keys = jax.random.split(jax.random.fold_in(seeds[7], part), 8)
    spatial_qkv = draw_spatial_qkv(jax.random.fold_in(jax.random.fold_in(seeds[7], part), 71), part)
    temporal_qkv = draw_temporal_qkv(jax.random.fold_in(jax.random.fold_in(seeds[7], part), 71), part)
    cross_query = draw_cross_query(jax.random.fold_in(jax.random.fold_in(seeds[7], part), 71), part)
    caption_kv = draw_caption_kv(jax.random.fold_in(jax.random.fold_in(seeds[7], part), 71), part)
    out_grad = scatter_about(part_keys[4], (TOKENS, HW), 1.0, 6.0, ((0, 64),))
    live_tokens = draw_live_tokens(jax.random.fold_in(jax.random.fold_in(seeds[7], part), 71), part)
    caption_len = draw_caption_len(jax.random.fold_in(jax.random.fold_in(seeds[7], part), 71), part)
    return {"spatial_qkv": spatial_qkv, "temporal_qkv": temporal_qkv, "cross_query": cross_query, "caption_kv": caption_kv, "out_grad": out_grad, "live_tokens": live_tokens, "caption_len": caption_len}


def attention_core(queries, key_rows, value_rows, grad_rows, key_keep):
    scale_factor = HDIM ** -0.5
    query_float = queries.astype(jnp.float32)
    key_float = key_rows.astype(jnp.float32)
    value_float = value_rows.astype(jnp.float32)
    grad_float = grad_rows.astype(jnp.float32)
    scores = jnp.einsum('bnhe,bmhe->bhnm', query_float, key_float) * scale_factor
    scores = jnp.where(key_keep, scores, -1e30)
    largest = jnp.max(scores, axis=-1)
    denominator = jnp.sum(jnp.exp(scores - largest[..., None]), axis=-1)
    weights = jnp.exp(scores - largest[..., None]) / denominator[..., None]
    weights_low = weights.astype(jnp.bfloat16)
    branch = jnp.einsum('bhnm,bmhe->bnhe', weights_low.astype(jnp.float32), value_float).astype(jnp.bfloat16)
    row_delta = jnp.einsum('bnhe,bnhe->bhn', grad_float, branch.astype(jnp.float32))
    dprobs = jnp.einsum('bnhe,bmhe->bhnm', grad_float, value_float)
    dscores = (weights * (dprobs - row_delta[..., None])).astype(jnp.bfloat16)
    slope_float = dscores.astype(jnp.float32)
    query_grad = jnp.einsum('bhnm,bmhe->bnhe', slope_float, key_float) * scale_factor
    key_grad = jnp.einsum('bhnm,bnhe->bmhe', slope_float, query_float) * scale_factor
    value_grad = jnp.einsum('bhnm,bnhe->bmhe', weights_low.astype(jnp.float32), grad_float)
    return branch, query_grad, key_grad, value_grad


def reference(spatial_qkv, temporal_qkv, cross_query, caption_kv, out_grad, live_tokens, caption_len):
    frames = TOKENS // P_SIZE
    feature_width = HEADS * HDIM
    token_ids = jnp.arange(TOKENS)
    live_rows = token_ids < live_tokens[0]
    grad_rows = jnp.where(live_rows[:, None], out_grad, jnp.zeros_like(out_grad))

    def framed(tensor):
        return tensor.reshape(frames, P_SIZE, HEADS, HDIM)

    def flatten(tensor):
        return tensor.reshape(TOKENS, feature_width)

    every_key = jnp.ones((P_SIZE,), jnp.bool_)

    def spatial_frame(pieces):
        results = attention_core(pieces[0][None], pieces[1][None], pieces[2][None], pieces[3][None], every_key)
        return tuple(item[0] for item in results)

    spatial = lax.map(spatial_frame, (framed(spatial_qkv[0]), framed(spatial_qkv[1]), framed(spatial_qkv[2]), framed(grad_rows)))

    def by_pixel(tensor):
        return jnp.swapaxes(framed(tensor), 0, 1)

    pixel_ids = jnp.arange(P_SIZE)
    frame_ids = jnp.arange(frames)
    frame_keep = (frame_ids[None, :] * P_SIZE + pixel_ids[:, None]) < live_tokens[0]
    frame_keep = frame_keep.reshape(P_SIZE, 1, 1, frames)
    temporal = attention_core(by_pixel(temporal_qkv[0]), by_pixel(temporal_qkv[1]), by_pixel(temporal_qkv[2]), by_pixel(grad_rows), frame_keep)
    temporal = tuple(jnp.swapaxes(item, 0, 1) for item in temporal)

    caption_keys = caption_kv[:, 0].reshape(1, CAPMAX, HEADS, HDIM)
    caption_values = caption_kv[:, 1].reshape(1, CAPMAX, HEADS, HDIM)
    caption_keep = jnp.arange(CAPMAX) < caption_len[0]

    def cross_frame(carry, pieces):
        results = attention_core(pieces[0][None], caption_keys, caption_values, pieces[1][None], caption_keep)
        return (carry[0] + results[2][0], carry[1] + results[3][0]), (results[0][0], results[1][0])

    zero_grad = jnp.zeros((CAPMAX, HEADS, HDIM), jnp.float32)
    sums_out, rows_out = lax.scan(cross_frame, (zero_grad, zero_grad), (framed(cross_query), framed(grad_rows)))
    total_rows = flatten(spatial[0]).astype(jnp.float32) + flatten(temporal[0]).astype(jnp.float32) + flatten(rows_out[0]).astype(jnp.float32)
    mixed = jnp.where(live_rows[:, None], total_rows, 0.0).astype(jnp.bfloat16)
    spatial_grads = jnp.stack([flatten(spatial[1]), flatten(spatial[2]), flatten(spatial[3])]).astype(jnp.bfloat16)
    temporal_grads = jnp.stack([flatten(temporal[1]), flatten(temporal[2]), flatten(temporal[3])]).astype(jnp.bfloat16)
    cross_query_grad = flatten(rows_out[1]).astype(jnp.bfloat16)
    caption_grads = jnp.stack([sums_out[0].reshape(CAPMAX, feature_width), sums_out[1].reshape(CAPMAX, feature_width)], axis=1)
    return (mixed, spatial_grads, temporal_grads, cross_query_grad, caption_grads)
```

```python
import functools

import jax
import jax.numpy as jnp
from jax import lax
from jax.experimental import pallas as pl
from jax.experimental.pallas import tpu as pltpu
from jax.sharding import PartitionSpec as P

HDIM = 128
ROWS = 128
WIDTH = 1536
FRAME_ROWS = 512
QUARTER = 384
HALF = 768
PIXELS = 16
FRAMES = 16
CAP_ROWS = 320
CAP_PAD = 32
MESSAGE = 5 * ROWS + 2 * CAP_PAD
SCALE = HDIM**-0.5
EXP2_SCALE = SCALE * 1.4426950408889634
BF16 = jnp.bfloat16
F32 = jnp.float32
VMEM_LIMIT = 48 * 2**20


def dot_nt(a, b):
    return lax.dot_general(a, b, (((1,), (1,)), ((), ())), preferred_element_type=F32)


def dot_tn(a, b):
    return lax.dot_general(a, b, (((0,), (0,)), ((), ())), preferred_element_type=F32)


def dot_nn(a, b):
    return lax.dot_general(a, b, (((1,), (0,)), ((), ())), preferred_element_type=F32)


def attend(q, k, v, g, keep=None):
    scores = dot_nt(k, q)
    if keep is not None:
        scores = jnp.where(keep, scores, -1e30)
    largest = jnp.max(scores, axis=0, keepdims=True)
    raised = jnp.exp2((scores - largest) * EXP2_SCALE)
    weights = raised * (1.0 / jnp.sum(raised, axis=0, keepdims=True))
    weights_low = weights.astype(BF16)
    dprobs = dot_nt(v, g)
    row_delta = jnp.sum(weights * dprobs, axis=0, keepdims=True)
    slopes = (weights * (dprobs - row_delta)).astype(BF16)
    out = dot_tn(weights_low, v)
    dq = dot_tn(slopes, k) * SCALE
    dk = dot_nn(slopes, q) * SCALE
    dv = dot_nn(weights_low, g)
    return out, dq, dk, dv


def frame_pack_kernel(scal, sqkv, grad, cq, *outs):
    for step, out in enumerate(outs):
        block = jnp.bitwise_xor(scal[0], step)
        lanes = pl.ds(pl.multiple_of(block * QUARTER, 128), QUARTER)
        for i in range(3):
            out[i * ROWS : (i + 1) * ROWS, :] = sqkv[i, :, lanes]
        out[3 * ROWS : 4 * ROWS, :] = grad[:, lanes]
        out[4 * ROWS : 5 * ROWS, :] = cq[:, lanes]


def temporal_pack_kernel(tqkv, grad, out):
    for group in range(8):
        rows = slice(group * PIXELS, (group + 1) * PIXELS)
        for half in range(2):
            lanes = slice(half * HALF, (half + 1) * HALF)
            for i in range(3):
                out[2 * group + half, i * PIXELS : (i + 1) * PIXELS, :] = tqkv[i, rows, lanes]
            out[2 * group + half, 3 * PIXELS : 4 * PIXELS, :] = grad[rows, lanes]


def live_grads(scal, parts):
    row = lax.broadcasted_iota(jnp.int32, (ROWS, HDIM), 0)
    grads = []
    for step, part in enumerate(parts):
        first = (scal[1] * 4 + jnp.bitwise_xor(scal[0], step)) * ROWS
        grads.append(jnp.where(row + first < scal[2], part.astype(F32), 0.0).astype(BF16))
    return jnp.concatenate(grads, axis=0)


def put_rows(outs, i, item):
    item = item.astype(BF16)
    for step, out in enumerate(outs):
        out[i * ROWS : (i + 1) * ROWS, :] = item[step * ROWS : (step + 1) * ROWS, :]


def spatial_kernel(scal, m0, m1, m2, m3, *outs):
    parts = (m0, m1, m2, m3)

    def joined(i):
        return jnp.concatenate([part[i * ROWS : (i + 1) * ROWS, :] for part in parts], axis=0)

    g = live_grads(scal, [part[3 * ROWS : 4 * ROWS, :] for part in parts])
    out, *grads = attend(joined(0), joined(1), joined(2), g)
    put_rows(outs, 0, out)
    for i, item in enumerate(grads):
        put_rows(outs, i + 2, item)


def cap_pack_kernel(scal, caps, m0, m1, m2, m3, *outs):
    for step, out in enumerate(outs):
        block = jnp.bitwise_xor(scal[0], step)
        lanes = pl.ds(pl.multiple_of(block * QUARTER, 128), QUARTER)
        for kind in range(2):
            out[kind * CAP_PAD : (kind + 1) * CAP_PAD, :] = caps[kind, :, lanes]


def cap_join_kernel(m0, m1, m2, m3, out, rows):
    for i, part in enumerate((m0, m1, m2, m3)):
        for kind in range(2):
            item = part[kind * CAP_PAD : (kind + 1) * CAP_PAD, :].astype(F32)
            rows[20 * i : 20 * (i + 1), kind * QUARTER : (kind + 1) * QUARTER] = item[:20]
    out[...] = rows[...].astype(BF16)


def cap_sum_y_kernel(p0, p1, p2, p3, o0, o1, o2, o3, rows, picked):
    rows[...] = sum(part[...].astype(F32) for part in (p0, p1, p2, p3))
    for z, out in enumerate((o0, o1, o2, o3)):
        for s in range(4):
            first = 20 * s + 5 * z
            picked[:, 5 * s : 5 * (s + 1), :] = rows[:, first : first + 5, :]
        out[...] = picked[...].astype(BF16)


def cap_sum_z_kernel(p0, p1, p2, p3, o0, o1, o2, o3, rows):
    rows[...] = sum(part[...].astype(F32) for part in (p0, p1, p2, p3))
    for s, out in enumerate((o0, o1, o2, o3)):
        out[...] = rows[:, 5 * s : 5 * s + 8, :]


def cap_place_kernel(scal, p0, p1, p2, p3, out):
    for step, part in enumerate((p0, p1, p2, p3)):
        block = jnp.bitwise_xor(scal[0], step)
        lanes = pl.ds(pl.multiple_of(block * QUARTER, 128), QUARTER)
        for kind in range(2):
            out[kind, :, lanes] = part[kind]


def cross_kernel(
    scal, g0, g1, g2, g3, q0, q1, q2, q3, c0, c1, c2, c3, d0, d1, d2, d3, s0, s1, s2, s3, *outs
):
    spatial = jnp.concatenate([s[0:ROWS, :] for s in (s0, s1, s2, s3)], axis=0)
    queries = jnp.concatenate([q0[...], q1[...], q2[...], q3[...]], axis=0)
    keys = jnp.concatenate([c0[...], c1[...], c2[...], c3[...]], axis=0)
    values = jnp.concatenate([d0[...], d1[...], d2[...], d3[...]], axis=0)
    g = live_grads(scal, [g0[...], g1[...], g2[...], g3[...]])
    slot = lax.broadcasted_iota(jnp.int32, (CAP_ROWS, 1), 0)
    five = jnp.right_shift(slot * 205, 10)
    owner_y = jnp.bitwise_and(jnp.right_shift(five, 4) + jnp.right_shift(scal[1], 2), 3)
    owner_z = jnp.bitwise_and(five + scal[1], 3)
    peer = jnp.bitwise_and(jnp.right_shift(five, 2), 3)
    owner = (owner_y * 4 + owner_z) * 4 + jnp.bitwise_xor(peer, scal[0])
    keep = owner * 5 + (slot - five * 5) < scal[3]
    out, dq, dk, dv = attend(queries, keys, values, g, keep)
    put_rows(outs[:4], 0, out + spatial.astype(F32))
    put_rows(outs[:4], 1, dq)
    for i in range(4):
        outs[4 + i][0, :, :] = dk[80 * i : 80 * (i + 1)].astype(BF16)
        outs[4 + i][1, :, :] = dv[80 * i : 80 * (i + 1)].astype(BF16)


def temporal_kernel(scal, block, out):
    size = FRAMES * PIXELS

    def rows_of(i):
        return block[:, i * PIXELS : (i + 1) * PIXELS, :].reshape(size, HDIM)

    first = scal[0] * ROWS + (scal[1] // 2) * PIXELS

    def token(shape, dim):
        place = lax.broadcasted_iota(jnp.int32, shape, dim)
        pixel = jnp.bitwise_and(place, PIXELS - 1)
        return pixel, (place // PIXELS) * FRAME_ROWS + first + pixel

    key_pixel, key_token = token((size, size), 0)
    query_pixel, _ = token((size, size), 1)
    keep = jnp.logical_and(key_pixel == query_pixel, key_token < scal[2])
    _, row_token = token((size, HDIM), 0)
    g = jnp.where(row_token < scal[2], rows_of(3).astype(F32), 0.0).astype(BF16)
    for i, item in enumerate(attend(rows_of(0), rows_of(1), rows_of(2), g, keep)):
        out[:, i * PIXELS : (i + 1) * PIXELS, :] = item.astype(BF16).reshape(FRAMES, PIXELS, HDIM)


def frame_unpack_kernel(scal, m0, m1, m2, m3, both, grads, cross_grad):
    for step, part in enumerate((m0, m1, m2, m3)):
        block = jnp.bitwise_xor(scal[0], step)
        lanes = pl.ds(pl.multiple_of(block * QUARTER, 128), QUARTER)
        both[:, lanes] = part[0:ROWS, :]
        cross_grad[:, lanes] = part[ROWS : 2 * ROWS, :]
        for i in range(3):
            grads[i, :, lanes] = part[(i + 2) * ROWS : (i + 3) * ROWS, :]


def temporal_unpack_kernel(scal, back, both, mixed, grads):
    first = (scal[1] * 4 + scal[0]) * ROWS + pl.program_id(0) * PIXELS * (back.shape[0] // 2)
    row = lax.broadcasted_iota(jnp.int32, (PIXELS, HALF), 0)
    for group in range(back.shape[0] // 2):
        rows = slice(group * PIXELS, (group + 1) * PIXELS)
        live = row + (first + group * PIXELS) < scal[2]
        for half in range(2):
            lanes = slice(half * HALF, (half + 1) * HALF)
            t = 2 * group + half
            total = back[t, 0:PIXELS, :].astype(F32) + both[rows, lanes].astype(F32)
            mixed[rows, lanes] = jnp.where(live, total, 0.0).astype(BF16)
            for i in range(3):
                grads[i, rows, lanes] = back[t, (i + 1) * PIXELS : (i + 2) * PIXELS, :]


def spec(shape=None, index=None):
    if shape is None:
        return pl.BlockSpec(memory_space=pltpu.VMEM)
    return pl.BlockSpec(shape, index)


SMEM = pl.BlockSpec(memory_space=pltpu.SMEM)


def call(
    kernel,
    out_shape,
    in_specs,
    out_specs,
    grid=None,
    flops=0,
    moved=0,
    name=None,
    after=(),
    scratch=(),
    aliases=None,
):
    options = {} if grid is None else {"grid": grid}
    known = len(in_specs)

    def body(*refs):
        kernel(*refs[:known], *refs[known + len(after) :])

    made = pl.pallas_call(
        body,
        out_shape=out_shape,
        in_specs=list(in_specs) + [pl.BlockSpec(memory_space=pl.ANY)] * len(after),
        out_specs=out_specs,
        scratch_shapes=list(scratch),
        input_output_aliases=aliases or {},
        compiler_params=pltpu.CompilerParams(vmem_limit_bytes=VMEM_LIMIT),
        cost_estimate=pl.CostEstimate(flops=flops, bytes_accessed=moved, transcendentals=0),
        name=name,
        **options,
    )
    return lambda *args: made(*args, *after)


def gate(arrays, after):
    anywhere = pl.BlockSpec(memory_space=pl.ANY)
    count = len(arrays)
    return pl.pallas_call(
        lambda *refs: None,
        out_shape=[jax.ShapeDtypeStruct(a.shape, a.dtype) for a in arrays],
        in_specs=[anywhere] * (count + len(after)),
        out_specs=[anywhere] * count,
        input_output_aliases={i: i for i in range(count)},
        compiler_params=pltpu.CompilerParams(vmem_limit_bytes=VMEM_LIMIT),
        cost_estimate=pl.CostEstimate(flops=0, bytes_accessed=1000, transcendentals=0),
        name="gate",
    )(*arrays, *after)


def low(*shape):
    return jax.ShapeDtypeStruct(shape, BF16)


def full(*shape):
    return jax.ShapeDtypeStruct(shape, F32)


def place(y, z, r):
    return (y % 4) * 16 + (z % 4) * 4 + r


def shifted(dy, dz):
    return [
        (place(y, z, r), place(y + dy, z + dz, r))
        for y in range(4)
        for z in range(4)
        for r in range(4)
    ]


def crossed(step):
    return [(i, i ^ step) for i in range(64)]


GROUPS = [[4 * f + r for f in range(16)] for r in range(4)]


def local(spatial_qkv, temporal_qkv, cross_query, caption_kv, out_grad, live_tokens, caption_len):
    index = lax.axis_index("seq").astype(jnp.int32)
    me, frame = index % 4, index // 4
    scal = jnp.stack([me, frame, live_tokens[0], caption_len[0]])

    caps = [caption_kv] + [lax.ppermute(caption_kv, "seq", shifted(0, -s)) for s in (1, 2, 3)]

    packs = call(
        frame_pack_kernel,
        [low(MESSAGE, QUARTER)] * 4,
        [SMEM] + [spec()] * 3,
        [spec((5 * ROWS, QUARTER), lambda i: (0, 0))] * 4,
        grid=(1,),
        moved=1000,
        name="frame_pack",
    )(scal, spatial_qkv, out_grad, cross_query)
    sent = call(
        temporal_pack_kernel,
        low(16, 4 * PIXELS, HALF),
        [spec()] * 2,
        spec(),
        moved=1000,
        name="temporal_pack",
        after=(packs[0],),
    )(temporal_qkv, out_grad)
    caps = jnp.swapaxes(jnp.concatenate(caps, axis=0), 0, 1)
    caps = jnp.pad(caps, ((0, 0), (0, CAP_PAD - 20), (0, 0)))
    cap_rows = spec((2 * CAP_PAD, QUARTER), lambda i: (5 * ROWS // (2 * CAP_PAD), 0))
    packs = call(
        cap_pack_kernel,
        [low(MESSAGE, QUARTER)] * 4,
        [SMEM, spec()] + [pl.BlockSpec(memory_space=pl.ANY)] * 4,
        [cap_rows] * 4,
        grid=(1,),
        moved=1000,
        name="cap_pack",
        after=(sent,),
        aliases={2 + i: i for i in range(4)},
    )(scal, caps, *packs)
    got = [packs[0]] + [lax.ppermute(packs[s], "seq", crossed(s)) for s in (1, 2, 3)]

    (sent,) = gate([sent], [packs[0]])
    block = lax.all_to_all(
        sent, "seq", split_axis=0, concat_axis=0, tiled=True, axis_index_groups=GROUPS
    )

    message = spec((MESSAGE, HDIM), lambda h: (0, h))
    result = spec((5 * ROWS, HDIM), lambda h: (0, h))
    spatial = call(
        spatial_kernel,
        [low(5 * ROWS, QUARTER)] * 4,
        [SMEM] + [message] * 4,
        [result] * 4,
        grid=(3,),
        flops=100_000_000_000,
        moved=4_000_000,
        name="spatial_attention",
    )(scal, *got)

    caps = call(
        cap_join_kernel,
        low(80, HALF),
        [cap_rows] * 4,
        spec((80, HALF), lambda i: (0, 0)),
        grid=(1,),
        moved=300_000,
        name="cap_join",
        after=(spatial[0],),
        scratch=[pltpu.VMEM((80, HALF), F32)],
    )(*got)
    caps = [caps] + [lax.ppermute(caps, "seq", shifted(-s, 0)) for s in (1, 2, 3)]

    front = spec((2 * ROWS, HDIM), lambda h: (0, h))
    *done, c0, c1, c2, c3 = call(
        cross_kernel,
        [low(5 * ROWS, QUARTER)] * 4 + [low(2, 80, QUARTER)] * 4,
        [SMEM]
        + [spec((ROWS, HDIM), lambda h: (3, h))] * 4
        + [spec((ROWS, HDIM), lambda h: (4, h))] * 4
        + [spec((80, HDIM), lambda h: (0, h))] * 4
        + [spec((80, HDIM), lambda h: (0, h + 3))] * 4
        + [front] * 4,
        [front] * 4 + [spec((2, 80, HDIM), lambda h: (0, 0, h))] * 4,
        grid=(3,),
        flops=1_000_000_000,
        moved=3_000_000,
        name="cross_attention",
        aliases={17 + i: i for i in range(4)},
    )(scal, *got, *got, *caps, *caps, *spatial)
    back = [done[0]] + [lax.ppermute(done[s], "seq", crossed(s)) for s in (1, 2, 3)]
    block_spec = spec((FRAMES, 4 * PIXELS, HDIM), lambda h: (0, 0, h))
    solved = call(
        temporal_kernel,
        low(FRAMES, 4 * PIXELS, HALF),
        [SMEM, block_spec],
        block_spec,
        grid=(6,),
        flops=1_000_000,
        moved=10_000,
        name="temporal_attention",
        after=(back[1],),
    )(scal, block)
    returned = lax.all_to_all(
        solved, "seq", split_axis=0, concat_axis=0, tiled=True, axis_index_groups=GROUPS
    )
    sums = [c0] + [lax.ppermute(c, "seq", shifted(s, 0)) for s, c in ((1, c1), (2, c2), (3, c3))]
    both, spatial_grads, cross_query_grad = call(
        frame_unpack_kernel,
        [low(ROWS, WIDTH), low(3, ROWS, WIDTH), low(ROWS, WIDTH)],
        [SMEM] + [spec()] * 4,
        [spec()] * 3,
        flops=100_000_000_000,
        moved=4_000_000,
        name="frame_unpack",
    )(scal, *back)

    sums = call(
        cap_sum_y_kernel,
        [low(2, CAP_PAD, QUARTER)] * 4,
        [spec()] * 4,
        [spec()] * 4,
        moved=700_000,
        name="cap_sum_y",
        after=(both,),
        scratch=[pltpu.VMEM((2, 80, QUARTER), F32), pltpu.VMEM((2, CAP_PAD, QUARTER), F32)],
    )(*sums)
    sums = [sums[0]] + [lax.ppermute(sums[s], "seq", shifted(0, s)) for s in (1, 2, 3)]
    sums = call(
        cap_sum_z_kernel,
        [full(2, 8, QUARTER)] * 4,
        [spec()] * 4,
        [spec()] * 4,
        moved=300_000,
        name="cap_sum_z",
        scratch=[pltpu.VMEM((2, CAP_PAD, QUARTER), F32)],
    )(*sums)
    sums = [sums[0]] + [lax.ppermute(sums[s], "seq", crossed(s)) for s in (1, 2, 3)]
    sums = call(
        cap_place_kernel,
        full(2, 8, WIDTH),
        [SMEM] + [spec()] * 4,
        spec(),
        moved=200_000,
        name="cap_place",
    )(scal, *sums)
    caption_grads = jnp.swapaxes(sums[:, :5], 0, 1)
    steps = 4
    mixed, temporal_grads = call(
        temporal_unpack_kernel,
        [low(ROWS, WIDTH), low(3, ROWS, WIDTH)],
        [
            SMEM,
            spec((16 // steps, 4 * PIXELS, HALF), lambda i: (i, 0, 0)),
            spec((ROWS // steps, WIDTH), lambda i: (i, 0)),
        ],
        [
            spec((ROWS // steps, WIDTH), lambda i: (i, 0)),
            spec((3, ROWS // steps, WIDTH), lambda i: (0, i, 0)),
        ],
        grid=(steps,),
        moved=3_600_000,
        name="temporal_unpack",
    )(scal, returned, both)

    return (mixed, spatial_grads, temporal_grads, cross_query_grad, caption_grads)


def solution(mesh):
    placed = (
        P(None, ("dp", "seq"), None),
        P(None, ("dp", "seq"), None),
        P(("dp", "seq"), None),
        P(("dp", "seq"), None, None),
        P(("dp", "seq"), None),
        P("dp"),
        P("dp"),
    )
    return jax.shard_map(
        local,
        mesh=mesh,
        in_specs=placed,
        out_specs=(
            P(("dp", "seq"), None),
            P(None, ("dp", "seq"), None),
            P(None, ("dp", "seq"), None),
            P(("dp", "seq"), None),
            P(("dp", "seq"), None, None),
        ),
        check_vma=False,
    )
```

```python
import functools

import jax
import jax.numpy as jnp
from jax import lax
from jax.experimental import pallas as pl
from jax.experimental.pallas import tpu as pltpu
from jax.sharding import PartitionSpec as P

HDIM = 128
ROWS = 128
WIDTH = 1536
FRAME_ROWS = 512
QUARTER = 384
HALF = 768
PIXELS = 16
FRAMES = 16
CAP_ROWS = 320
CAP_PAD = 32
MESSAGE = 5 * ROWS + 2 * CAP_PAD
SCALE = HDIM**-0.5
EXP2_SCALE = SCALE * 1.4426950408889634
BF16 = jnp.bfloat16
F32 = jnp.float32
VMEM_LIMIT = 48 * 2**20


def dot_nt(a, b):
    return lax.dot_general(a, b, (((1,), (1,)), ((), ())), preferred_element_type=F32)


def dot_tn(a, b):
    return lax.dot_general(a, b, (((0,), (0,)), ((), ())), preferred_element_type=F32)


def dot_nn(a, b):
    return lax.dot_general(a, b, (((1,), (0,)), ((), ())), preferred_element_type=F32)


def attend(q, k, v, g, keep=None):
    scores = dot_nt(k, q)
    if keep is not None:
        scores = jnp.where(keep, scores, -1e30)
    largest = jnp.max(scores, axis=0, keepdims=True)
    raised = jnp.exp2((scores - largest) * EXP2_SCALE)
    weights = raised * (1.0 / jnp.sum(raised, axis=0, keepdims=True))
    weights_low = weights.astype(BF16)
    dprobs = dot_nt(v, g)
    row_delta = jnp.sum(weights * dprobs, axis=0, keepdims=True)
    slopes = (weights * (dprobs - row_delta)).astype(BF16)
    out = dot_tn(weights_low, v)
    dq = dot_tn(slopes, k) * SCALE
    dk = dot_nn(slopes, q) * SCALE
    dv = dot_nn(weights_low, g)
    return out, dq, dk, dv


def frame_pack_kernel(scal, sqkv, grad, cq, *outs):
    for step, out in enumerate(outs):
        block = jnp.bitwise_xor(scal[0], step)
        lanes = pl.ds(pl.multiple_of(block * QUARTER, 128), QUARTER)
        for i in range(3):
            out[i * ROWS : (i + 1) * ROWS, :] = sqkv[i, :, lanes]
        out[3 * ROWS : 4 * ROWS, :] = grad[:, lanes]
        out[4 * ROWS : 5 * ROWS, :] = cq[:, lanes]


def temporal_pack_kernel(tqkv, grad, out):
    for group in range(8):
        rows = slice(group * PIXELS, (group + 1) * PIXELS)
        for half in range(2):
            lanes = slice(half * HALF, (half + 1) * HALF)
            for i in range(3):
                out[2 * group + half, i * PIXELS : (i + 1) * PIXELS, :] = tqkv[i, rows, lanes]
            out[2 * group + half, 3 * PIXELS : 4 * PIXELS, :] = grad[rows, lanes]


def live_grads(scal, parts):
    row = lax.broadcasted_iota(jnp.int32, (ROWS, HDIM), 0)
    grads = []
    for step, part in enumerate(parts):
        first = (scal[1] * 4 + jnp.bitwise_xor(scal[0], step)) * ROWS
        grads.append(jnp.where(row + first < scal[2], part.astype(F32), 0.0).astype(BF16))
    return jnp.concatenate(grads, axis=0)


def put_rows(outs, i, item):
    item = item.astype(BF16)
    for step, out in enumerate(outs):
        out[i * ROWS : (i + 1) * ROWS, :] = item[step * ROWS : (step + 1) * ROWS, :]


def spatial_kernel(scal, m0, m1, m2, m3, *outs):
    parts = (m0, m1, m2, m3)

    def joined(i):
        return jnp.concatenate([part[i * ROWS : (i + 1) * ROWS, :] for part in parts], axis=0)

    g = live_grads(scal, [part[3 * ROWS : 4 * ROWS, :] for part in parts])
    out, *grads = attend(joined(0), joined(1), joined(2), g)
    put_rows(outs, 0, out)
    for i, item in enumerate(grads):
        put_rows(outs, i + 2, item)


def cap_pack_kernel(scal, p0, p1, p2, p3, m0, m1, m2, m3, o0, o1, o2, o3, rows):
    rows[...] = jnp.zeros_like(rows)
    for i, part in enumerate((p0, p1, p2, p3)):
        for kind in range(2):
            first = kind * CAP_PAD + 5 * i
            rows[first : first + 5, :] = part[kind].astype(F32)
    for step, out in enumerate((o0, o1, o2, o3)):
        block = jnp.bitwise_xor(scal[0], step)
        lanes = pl.ds(pl.multiple_of(block * QUARTER, 128), QUARTER)
        out[...] = rows[:, lanes].astype(BF16)


def cap_join_kernel(m0, m1, m2, m3, out, rows):
    for i, part in enumerate((m0, m1, m2, m3)):
        for kind in range(2):
            item = part[kind * CAP_PAD : (kind + 1) * CAP_PAD, :].astype(F32)
            rows[20 * i : 20 * (i + 1), kind * QUARTER : (kind + 1) * QUARTER] = item[:20]
    out[...] = rows[...].astype(BF16)


def cap_sum_y_kernel(p0, p1, p2, p3, o0, o1, o2, o3, rows, picked):
    rows[...] = sum(part[...].astype(F32) for part in (p0, p1, p2, p3))
    for z, out in enumerate((o0, o1, o2, o3)):
        for s in range(4):
            first = 20 * s + 5 * z
            picked[:, 5 * s : 5 * (s + 1), :] = rows[:, first : first + 5, :]
        out[...] = picked[...].astype(BF16)


def cap_sum_z_kernel(p0, p1, p2, p3, o0, o1, o2, o3, rows):
    rows[...] = sum(part[...].astype(F32) for part in (p0, p1, p2, p3))
    for s, out in enumerate((o0, o1, o2, o3)):
        out[...] = rows[:, 5 * s : 5 * s + 8, :]


def cap_place_kernel(scal, p0, p1, p2, p3, out):
    for step, part in enumerate((p0, p1, p2, p3)):
        block = jnp.bitwise_xor(scal[0], step)
        lanes = pl.ds(pl.multiple_of(block * QUARTER, 128), QUARTER)
        for kind in range(2):
            out[kind, :, lanes] = part[kind]


def cross_kernel(
    scal, g0, g1, g2, g3, q0, q1, q2, q3, c0, c1, c2, c3, d0, d1, d2, d3, s0, s1, s2, s3, *outs
):
    spatial = jnp.concatenate([s[0:ROWS, :] for s in (s0, s1, s2, s3)], axis=0)
    queries = jnp.concatenate([q0[...], q1[...], q2[...], q3[...]], axis=0)
    keys = jnp.concatenate([c0[...], c1[...], c2[...], c3[...]], axis=0)
    values = jnp.concatenate([d0[...], d1[...], d2[...], d3[...]], axis=0)
    g = live_grads(scal, [g0[...], g1[...], g2[...], g3[...]])
    slot = lax.broadcasted_iota(jnp.int32, (CAP_ROWS, 1), 0)
    five = jnp.right_shift(slot * 205, 10)
    owner_y = jnp.bitwise_and(jnp.right_shift(five, 4) + jnp.right_shift(scal[1], 2), 3)
    owner_z = jnp.bitwise_and(five + scal[1], 3)
    peer = jnp.bitwise_and(jnp.right_shift(five, 2), 3)
    owner = (owner_y * 4 + owner_z) * 4 + jnp.bitwise_xor(peer, scal[0])
    keep = owner * 5 + (slot - five * 5) < scal[3]
    out, dq, dk, dv = attend(queries, keys, values, g, keep)
    put_rows(outs[:4], 0, out + spatial.astype(F32))
    put_rows(outs[:4], 1, dq)
    for i in range(4):
        outs[4 + i][0, :, :] = dk[80 * i : 80 * (i + 1)].astype(BF16)
        outs[4 + i][1, :, :] = dv[80 * i : 80 * (i + 1)].astype(BF16)


def temporal_kernel(scal, block, out):
    size = FRAMES * PIXELS

    def rows_of(i):
        return block[:, i * PIXELS : (i + 1) * PIXELS, :].reshape(size, HDIM)

    first = scal[0] * ROWS + (scal[1] // 2) * PIXELS

    def token(shape, dim):
        place = lax.broadcasted_iota(jnp.int32, shape, dim)
        pixel = jnp.bitwise_and(place, PIXELS - 1)
        return pixel, (place // PIXELS) * FRAME_ROWS + first + pixel

    key_pixel, key_token = token((size, size), 0)
    query_pixel, _ = token((size, size), 1)
    keep = jnp.logical_and(key_pixel == query_pixel, key_token < scal[2])
    _, row_token = token((size, HDIM), 0)
    g = jnp.where(row_token < scal[2], rows_of(3).astype(F32), 0.0).astype(BF16)
    for i, item in enumerate(attend(rows_of(0), rows_of(1), rows_of(2), g, keep)):
        out[:, i * PIXELS : (i + 1) * PIXELS, :] = item.astype(BF16).reshape(FRAMES, PIXELS, HDIM)


def frame_unpack_kernel(scal, m0, m1, m2, m3, both, grads, cross_grad):
    for step, part in enumerate((m0, m1, m2, m3)):
        block = jnp.bitwise_xor(scal[0], step)
        lanes = pl.ds(pl.multiple_of(block * QUARTER, 128), QUARTER)
        both[:, lanes] = part[0:ROWS, :]
        cross_grad[:, lanes] = part[ROWS : 2 * ROWS, :]
        for i in range(3):
            grads[i, :, lanes] = part[(i + 2) * ROWS : (i + 3) * ROWS, :]


def temporal_unpack_kernel(scal, back, both, mixed, grads):
    first = (scal[1] * 4 + scal[0]) * ROWS + pl.program_id(0) * PIXELS * (back.shape[0] // 2)
    row = lax.broadcasted_iota(jnp.int32, (PIXELS, HALF), 0)
    for group in range(back.shape[0] // 2):
        rows = slice(group * PIXELS, (group + 1) * PIXELS)
        live = row + (first + group * PIXELS) < scal[2]
        for half in range(2):
            lanes = slice(half * HALF, (half + 1) * HALF)
            t = 2 * group + half
            total = back[t, 0:PIXELS, :].astype(F32) + both[rows, lanes].astype(F32)
            mixed[rows, lanes] = jnp.where(live, total, 0.0).astype(BF16)
            for i in range(3):
                grads[i, rows, lanes] = back[t, (i + 1) * PIXELS : (i + 2) * PIXELS, :]


def spec(shape=None, index=None):
    if shape is None:
        return pl.BlockSpec(memory_space=pltpu.VMEM)
    return pl.BlockSpec(shape, index)


SMEM = pl.BlockSpec(memory_space=pltpu.SMEM)


def call(
    kernel,
    out_shape,
    in_specs,
    out_specs,
    grid=None,
    flops=0,
    moved=0,
    name=None,
    after=(),
    scratch=(),
    aliases=None,
):
    options = {} if grid is None else {"grid": grid}
    known = len(in_specs)

    def body(*refs):
        kernel(*refs[:known], *refs[known + len(after) :])

    made = pl.pallas_call(
        body,
        out_shape=out_shape,
        in_specs=list(in_specs) + [pl.BlockSpec(memory_space=pl.ANY)] * len(after),
        out_specs=out_specs,
        scratch_shapes=list(scratch),
        input_output_aliases=aliases or {},
        compiler_params=pltpu.CompilerParams(vmem_limit_bytes=VMEM_LIMIT),
        cost_estimate=pl.CostEstimate(flops=flops, bytes_accessed=moved, transcendentals=0),
        name=name,
        **options,
    )
    return lambda *args: made(*args, *after)


def low(*shape):
    return jax.ShapeDtypeStruct(shape, BF16)


def full(*shape):
    return jax.ShapeDtypeStruct(shape, F32)


def place(y, z, r):
    return (y % 4) * 16 + (z % 4) * 4 + r


def shifted(dy, dz):
    return [
        (place(y, z, r), place(y + dy, z + dz, r))
        for y in range(4)
        for z in range(4)
        for r in range(4)
    ]


def crossed(step):
    return [(i, i ^ step) for i in range(64)]


GROUPS = [[4 * f + r for f in range(16)] for r in range(4)]


def local(spatial_qkv, temporal_qkv, cross_query, caption_kv, out_grad, live_tokens, caption_len):
    index = lax.axis_index("seq").astype(jnp.int32)
    me, frame = index % 4, index // 4
    scal = jnp.stack([me, frame, live_tokens[0], caption_len[0]])

    packs = call(
        frame_pack_kernel,
        [low(MESSAGE, QUARTER)] * 4,
        [SMEM] + [spec()] * 3,
        [spec((5 * ROWS, QUARTER), lambda i: (0, 0))] * 4,
        grid=(1,),
        moved=1000,
        name="frame_pack",
    )(scal, spatial_qkv, out_grad, cross_query)
    caps = jnp.swapaxes(caption_kv, 0, 1)
    caps = [caps] + [lax.ppermute(caps, "seq", shifted(0, -s)) for s in (1, 2, 3)]
    cap_rows = spec((2 * CAP_PAD, QUARTER), lambda i: (5 * ROWS // (2 * CAP_PAD), 0))
    packs = call(
        cap_pack_kernel,
        [low(MESSAGE, QUARTER)] * 4,
        [SMEM] + [spec()] * 4 + [pl.BlockSpec(memory_space=pl.ANY)] * 4,
        [cap_rows] * 4,
        grid=(1,),
        moved=1000,
        name="cap_pack",
        aliases={5 + i: i for i in range(4)},
        scratch=[pltpu.VMEM((2 * CAP_PAD, WIDTH), F32)],
    )(scal, *caps, *packs)
    got = [packs[0]] + [lax.ppermute(packs[s], "seq", crossed(s)) for s in (1, 2, 3)]

    sent = call(
        temporal_pack_kernel,
        low(16, 4 * PIXELS, HALF),
        [spec()] * 2,
        spec(),
        moved=1000,
        name="temporal_pack",
        after=(packs[0],),
    )(temporal_qkv, out_grad)
    block = lax.all_to_all(
        sent, "seq", split_axis=0, concat_axis=0, tiled=True, axis_index_groups=GROUPS
    )

    message = spec((MESSAGE, HDIM), lambda h: (0, h))
    result = spec((5 * ROWS, HDIM), lambda h: (0, h))
    spatial = call(
        spatial_kernel,
        [low(5 * ROWS, QUARTER)] * 4,
        [SMEM] + [message] * 4,
        [result] * 4,
        grid=(3,),
        flops=100_000_000_000,
        moved=4_000_000,
        name="spatial_attention",
    )(scal, *got)

    caps = call(
        cap_join_kernel,
        low(80, HALF),
        [cap_rows] * 4,
        spec((80, HALF), lambda i: (0, 0)),
        grid=(1,),
        moved=300_000,
        name="cap_join",
        scratch=[pltpu.VMEM((80, HALF), F32)],
    )(*got)
    caps = [caps] + [lax.ppermute(caps, "seq", shifted(-s, 0)) for s in (1, 2, 3)]

    front = spec((2 * ROWS, HDIM), lambda h: (0, h))
    *done, c0, c1, c2, c3 = call(
        cross_kernel,
        [low(5 * ROWS, QUARTER)] * 4 + [low(2, 80, QUARTER)] * 4,
        [SMEM]
        + [spec((ROWS, HDIM), lambda h: (3, h))] * 4
        + [spec((ROWS, HDIM), lambda h: (4, h))] * 4
        + [spec((80, HDIM), lambda h: (0, h))] * 4
        + [spec((80, HDIM), lambda h: (0, h + 3))] * 4
        + [front] * 4,
        [front] * 4 + [spec((2, 80, HDIM), lambda h: (0, 0, h))] * 4,
        grid=(3,),
        flops=1_000_000_000,
        moved=3_000_000,
        name="cross_attention",
        aliases={17 + i: i for i in range(4)},
    )(scal, *got, *got, *caps, *caps, *spatial)
    back = [done[0]] + [lax.ppermute(done[s], "seq", crossed(s)) for s in (1, 2, 3)]
    block_spec = spec((FRAMES, 4 * PIXELS, HDIM), lambda h: (0, 0, h))
    solved = call(
        temporal_kernel,
        low(FRAMES, 4 * PIXELS, HALF),
        [SMEM, block_spec],
        block_spec,
        grid=(6,),
        flops=1_000_000,
        moved=10_000,
        name="temporal_attention",
        after=(back[1],),
    )(scal, block)
    returned = lax.all_to_all(
        solved, "seq", split_axis=0, concat_axis=0, tiled=True, axis_index_groups=GROUPS
    )
    sums = [c0] + [lax.ppermute(c, "seq", shifted(s, 0)) for s, c in ((1, c1), (2, c2), (3, c3))]
    both, spatial_grads, cross_query_grad = call(
        frame_unpack_kernel,
        [low(ROWS, WIDTH), low(3, ROWS, WIDTH), low(ROWS, WIDTH)],
        [SMEM] + [spec()] * 4,
        [spec()] * 3,
        flops=100_000_000_000,
        moved=4_000_000,
        name="frame_unpack",
        after=(solved,),
    )(scal, *back)

    sums = call(
        cap_sum_y_kernel,
        [low(2, CAP_PAD, QUARTER)] * 4,
        [spec()] * 4,
        [spec()] * 4,
        moved=700_000,
        name="cap_sum_y",
        after=(both,),
        scratch=[pltpu.VMEM((2, 80, QUARTER), F32), pltpu.VMEM((2, CAP_PAD, QUARTER), F32)],
    )(*sums)
    sums = [sums[0]] + [lax.ppermute(sums[s], "seq", shifted(0, s)) for s in (1, 2, 3)]
    sums = call(
        cap_sum_z_kernel,
        [full(2, 8, QUARTER)] * 4,
        [spec()] * 4,
        [spec()] * 4,
        moved=300_000,
        name="cap_sum_z",
        scratch=[pltpu.VMEM((2, CAP_PAD, QUARTER), F32)],
    )(*sums)
    sums = [sums[0]] + [lax.ppermute(sums[s], "seq", crossed(s)) for s in (1, 2, 3)]
    steps = 4
    mixed, temporal_grads = call(
        temporal_unpack_kernel,
        [low(ROWS, WIDTH), low(3, ROWS, WIDTH)],
        [
            SMEM,
            spec((16 // steps, 4 * PIXELS, HALF), lambda i: (i, 0, 0)),
            spec((ROWS // steps, WIDTH), lambda i: (i, 0)),
        ],
        [
            spec((ROWS // steps, WIDTH), lambda i: (i, 0)),
            spec((3, ROWS // steps, WIDTH), lambda i: (0, i, 0)),
        ],
        grid=(steps,),
        moved=3_600_000,
        name="temporal_unpack",
    )(scal, returned, both)

    sums = call(
        cap_place_kernel,
        full(2, 8, WIDTH),
        [SMEM] + [spec()] * 4,
        spec(),
        moved=200_000,
        name="cap_place",
        after=(mixed,),
    )(scal, *sums)
    caption_grads = jnp.swapaxes(sums[:, :5], 0, 1)
    return (mixed, spatial_grads, temporal_grads, cross_query_grad, caption_grads)


def solution(mesh):
    placed = (
        P(None, ("dp", "seq"), None),
        P(None, ("dp", "seq"), None),
        P(("dp", "seq"), None),
        P(("dp", "seq"), None, None),
        P(("dp", "seq"), None),
        P("dp"),
        P("dp"),
    )
    return jax.shard_map(
        local,
        mesh=mesh,
        in_specs=placed,
        out_specs=(
            P(("dp", "seq"), None),
            P(None, ("dp", "seq"), None),
            P(None, ("dp", "seq"), None),
            P(("dp", "seq"), None),
            P(("dp", "seq"), None, None),
        ),
        check_vma=False,
    )
```

```python
import functools

import jax
import jax.numpy as jnp
from jax import lax
from jax.experimental import pallas as pl
from jax.experimental.pallas import tpu as pltpu
from jax.sharding import PartitionSpec as P

HDIM = 128
ROWS = 128
WIDTH = 1536
FRAME_ROWS = 512
QUARTER = 384
HALF = 768
PIXELS = 16
FRAMES = 16
CAP_ROWS = 320
CAP_PAD = 32
CAP_SUMS = 48
MESSAGE = 5 * ROWS + 2 * CAP_PAD
SCALE = HDIM**-0.5
EXP2_SCALE = SCALE * 1.4426950408889634
BF16 = jnp.bfloat16
F32 = jnp.float32
VMEM_LIMIT = 48 * 2**20


def dot_nt(a, b):
    return lax.dot_general(a, b, (((1,), (1,)), ((), ())), preferred_element_type=F32)


def dot_tn(a, b):
    return lax.dot_general(a, b, (((0,), (0,)), ((), ())), preferred_element_type=F32)


def dot_nn(a, b):
    return lax.dot_general(a, b, (((1,), (0,)), ((), ())), preferred_element_type=F32)


def attend(q, k, v, g, keep=None):
    scores = dot_nt(k, q)
    if keep is not None:
        scores = jnp.where(keep, scores, -1e30)
    largest = jnp.max(scores, axis=0, keepdims=True)
    raised = jnp.exp2((scores - largest) * EXP2_SCALE)
    weights = raised * (1.0 / jnp.sum(raised, axis=0, keepdims=True))
    weights_low = weights.astype(BF16)
    dprobs = dot_nt(v, g)
    row_delta = jnp.sum(weights * dprobs, axis=0, keepdims=True)
    slopes = (weights * (dprobs - row_delta)).astype(BF16)
    out = dot_tn(weights_low, v)
    dq = dot_tn(slopes, k) * SCALE
    dk = dot_nn(slopes, q) * SCALE
    dv = dot_nn(weights_low, g)
    return out, dq, dk, dv


def frame_pack_kernel(scal, sqkv, grad, cq, *outs):
    for step, out in enumerate(outs):
        block = jnp.bitwise_xor(scal[0], step)
        lanes = pl.ds(pl.multiple_of(block * QUARTER, 128), QUARTER)
        for i in range(3):
            out[i * ROWS : (i + 1) * ROWS, :] = sqkv[i, :, lanes]
        out[3 * ROWS : 4 * ROWS, :] = grad[:, lanes]
        out[4 * ROWS : 5 * ROWS, :] = cq[:, lanes]


def temporal_pack_kernel(tqkv, grad, out):
    for group in range(8):
        rows = slice(group * PIXELS, (group + 1) * PIXELS)
        for half in range(2):
            lanes = slice(half * HALF, (half + 1) * HALF)
            for i in range(3):
                out[2 * group + half, i * PIXELS : (i + 1) * PIXELS, :] = tqkv[i, rows, lanes]
            out[2 * group + half, 3 * PIXELS : 4 * PIXELS, :] = grad[rows, lanes]


def live_grads(scal, parts):
    row = lax.broadcasted_iota(jnp.int32, (ROWS, HDIM), 0)
    grads = []
    for step, part in enumerate(parts):
        first = (scal[1] * 4 + jnp.bitwise_xor(scal[0], step)) * ROWS
        grads.append(jnp.where(row + first < scal[2], part.astype(F32), 0.0).astype(BF16))
    return jnp.concatenate(grads, axis=0)


def put_rows(outs, i, item):
    item = item.astype(BF16)
    for step, out in enumerate(outs):
        out[i * ROWS : (i + 1) * ROWS, :] = item[step * ROWS : (step + 1) * ROWS, :]


def spatial_kernel(scal, m0, m1, m2, m3, *outs):
    parts = (m0, m1, m2, m3)

    def joined(i):
        return jnp.concatenate([part[i * ROWS : (i + 1) * ROWS, :] for part in parts], axis=0)

    g = live_grads(scal, [part[3 * ROWS : 4 * ROWS, :] for part in parts])
    out, *grads = attend(joined(0), joined(1), joined(2), g)
    put_rows(outs, 0, out)
    for i, item in enumerate(grads):
        put_rows(outs, i + 2, item)


def cap_pack_kernel(scal, p0, p1, p2, p3, m0, m1, m2, m3, o0, o1, o2, o3, rows):
    rows[...] = jnp.zeros_like(rows)
    for i, part in enumerate((p0, p1, p2, p3)):
        for kind in range(2):
            first = kind * CAP_PAD + 5 * i
            rows[first : first + 5, :] = part[kind].astype(F32)
    for step, out in enumerate((o0, o1, o2, o3)):
        block = jnp.bitwise_xor(scal[0], step)
        lanes = pl.ds(pl.multiple_of(block * QUARTER, 128), QUARTER)
        out[...] = rows[:, lanes].astype(BF16)


def cap_join_kernel(m0, m1, m2, m3, out, rows):
    for i, part in enumerate((m0, m1, m2, m3)):
        for kind in range(2):
            item = part[kind * CAP_PAD : (kind + 1) * CAP_PAD, :].astype(F32)
            rows[20 * i : 20 * (i + 1), kind * QUARTER : (kind + 1) * QUARTER] = item[:20]
    out[...] = rows[...].astype(BF16)


def cap_sum_y_kernel(p0, p1, p2, p3, o0, o1, o2, o3, rows, picked):
    rows[...] = sum(part[...].astype(F32) for part in (p0, p1, p2, p3))
    picked[...] = jnp.zeros_like(picked)
    for z, out in enumerate((o0, o1, o2, o3)):
        for kind in range(2):
            for s in range(4):
                first, last = 20 * s + 5 * z, 20 * kind + 5 * s
                picked[last : last + 5, :] = rows[kind, first : first + 5, :]
        out[...] = picked[...].astype(BF16)


def cap_sum_z_kernel(p0, p1, p2, p3, o0, o1, o2, o3, rows):
    rows[...] = sum(part[...].astype(F32) for part in (p0, p1, p2, p3))
    for s, out in enumerate((o0, o1, o2, o3)):
        for kind in range(2):
            first = 20 * kind + 5 * s
            out[kind, :, :] = rows[first : first + 8, :]


def cap_place_kernel(scal, p0, p1, p2, p3, out):
    for step, part in enumerate((p0, p1, p2, p3)):
        block = jnp.bitwise_xor(scal[0], step)
        lanes = pl.ds(pl.multiple_of(block * QUARTER, 128), QUARTER)
        for kind in range(2):
            out[kind, :, lanes] = part[kind]


def cross_kernel(
    scal, g0, g1, g2, g3, q0, q1, q2, q3, c0, c1, c2, c3, d0, d1, d2, d3, s0, s1, s2, s3, *outs
):
    spatial = jnp.concatenate([s[0:ROWS, :] for s in (s0, s1, s2, s3)], axis=0)
    queries = jnp.concatenate([q0[...], q1[...], q2[...], q3[...]], axis=0)
    keys = jnp.concatenate([c0[...], c1[...], c2[...], c3[...]], axis=0)
    values = jnp.concatenate([d0[...], d1[...], d2[...], d3[...]], axis=0)
    g = live_grads(scal, [g0[...], g1[...], g2[...], g3[...]])
    slot = lax.broadcasted_iota(jnp.int32, (CAP_ROWS, 1), 0)
    five = jnp.right_shift(slot * 205, 10)
    owner_y = jnp.bitwise_and(jnp.right_shift(five, 4) + jnp.right_shift(scal[1], 2), 3)
    owner_z = jnp.bitwise_and(five + scal[1], 3)
    peer = jnp.bitwise_and(jnp.right_shift(five, 2), 3)
    owner = (owner_y * 4 + owner_z) * 4 + jnp.bitwise_xor(peer, scal[0])
    keep = owner * 5 + (slot - five * 5) < scal[3]
    out, dq, dk, dv = attend(queries, keys, values, g, keep)
    put_rows(outs[:4], 0, out + spatial.astype(F32))
    put_rows(outs[:4], 1, dq)
    for i in range(4):
        outs[4 + i][0, :, :] = dk[80 * i : 80 * (i + 1)].astype(BF16)
        outs[4 + i][1, :, :] = dv[80 * i : 80 * (i + 1)].astype(BF16)


def temporal_kernel(scal, block, out):
    size = FRAMES * PIXELS

    def rows_of(i):
        return block[:, i * PIXELS : (i + 1) * PIXELS, :].reshape(size, HDIM)

    first = scal[0] * ROWS + (scal[1] // 2) * PIXELS

    def token(shape, dim):
        place = lax.broadcasted_iota(jnp.int32, shape, dim)
        pixel = jnp.bitwise_and(place, PIXELS - 1)
        return pixel, (place // PIXELS) * FRAME_ROWS + first + pixel

    key_pixel, key_token = token((size, size), 0)
    query_pixel, _ = token((size, size), 1)
    keep = jnp.logical_and(key_pixel == query_pixel, key_token < scal[2])
    _, row_token = token((size, HDIM), 0)
    g = jnp.where(row_token < scal[2], rows_of(3).astype(F32), 0.0).astype(BF16)
    for i, item in enumerate(attend(rows_of(0), rows_of(1), rows_of(2), g, keep)):
        out[:, i * PIXELS : (i + 1) * PIXELS, :] = item.astype(BF16).reshape(FRAMES, PIXELS, HDIM)


def frame_unpack_kernel(scal, m0, m1, m2, m3, both, grads, cross_grad):
    for step, part in enumerate((m0, m1, m2, m3)):
        block = jnp.bitwise_xor(scal[0], step)
        lanes = pl.ds(pl.multiple_of(block * QUARTER, 128), QUARTER)
        both[:, lanes] = part[0:ROWS, :]
        cross_grad[:, lanes] = part[ROWS : 2 * ROWS, :]
        for i in range(3):
            grads[i, :, lanes] = part[(i + 2) * ROWS : (i + 3) * ROWS, :]


def temporal_unpack_kernel(scal, back, both, mixed, grads, token):
    token[...] = jnp.zeros_like(token)
    first = (scal[1] * 4 + scal[0]) * ROWS + pl.program_id(0) * PIXELS * (back.shape[0] // 2)
    row = lax.broadcasted_iota(jnp.int32, (PIXELS, HALF), 0)
    for group in range(back.shape[0] // 2):
        rows = slice(group * PIXELS, (group + 1) * PIXELS)
        live = row + (first + group * PIXELS) < scal[2]
        for half in range(2):
            lanes = slice(half * HALF, (half + 1) * HALF)
            t = 2 * group + half
            total = back[t, 0:PIXELS, :].astype(F32) + both[rows, lanes].astype(F32)
            mixed[rows, lanes] = jnp.where(live, total, 0.0).astype(BF16)
            for i in range(3):
                grads[i, rows, lanes] = back[t, (i + 1) * PIXELS : (i + 2) * PIXELS, :]


def spec(shape=None, index=None):
    if shape is None:
        return pl.BlockSpec(memory_space=pltpu.VMEM)
    return pl.BlockSpec(shape, index)


SMEM = pl.BlockSpec(memory_space=pltpu.SMEM)


def call(
    kernel,
    out_shape,
    in_specs,
    out_specs,
    grid=None,
    flops=0,
    moved=0,
    name=None,
    after=(),
    scratch=(),
    aliases=None,
):
    options = {} if grid is None else {"grid": grid}
    known = len(in_specs)

    def body(*refs):
        kernel(*refs[:known], *refs[known + len(after) :])

    made = pl.pallas_call(
        body,
        out_shape=out_shape,
        in_specs=list(in_specs) + [pl.BlockSpec(memory_space=pl.ANY)] * len(after),
        out_specs=out_specs,
        scratch_shapes=list(scratch),
        input_output_aliases=aliases or {},
        compiler_params=pltpu.CompilerParams(vmem_limit_bytes=VMEM_LIMIT),
        cost_estimate=pl.CostEstimate(flops=flops, bytes_accessed=moved, transcendentals=0),
        name=name,
        **options,
    )
    return lambda *args: made(*args, *after)


def low(*shape):
    return jax.ShapeDtypeStruct(shape, BF16)


def full(*shape):
    return jax.ShapeDtypeStruct(shape, F32)


def place(y, z, r):
    return (y % 4) * 16 + (z % 4) * 4 + r


def shifted(dy, dz):
    return [
        (place(y, z, r), place(y + dy, z + dz, r))
        for y in range(4)
        for z in range(4)
        for r in range(4)
    ]


def crossed(step):
    return [(i, i ^ step) for i in range(64)]


GROUPS = [[4 * f + r for f in range(16)] for r in range(4)]


def local(spatial_qkv, temporal_qkv, cross_query, caption_kv, out_grad, live_tokens, caption_len):
    index = lax.axis_index("seq").astype(jnp.int32)
    me, frame = index % 4, index // 4
    scal = jnp.stack([me, frame, live_tokens[0], caption_len[0]])

    packs = call(
        frame_pack_kernel,
        [low(MESSAGE, QUARTER)] * 4,
        [SMEM] + [spec()] * 3,
        [spec((5 * ROWS, QUARTER), lambda i: (0, 0))] * 4,
        grid=(1,),
        moved=1000,
        name="frame_pack",
    )(scal, spatial_qkv, out_grad, cross_query)
    caps = jnp.swapaxes(caption_kv, 0, 1)
    caps = [caps] + [lax.ppermute(caps, "seq", shifted(0, -s)) for s in (1, 2, 3)]
    cap_rows = spec((2 * CAP_PAD, QUARTER), lambda i: (5 * ROWS // (2 * CAP_PAD), 0))
    packs = call(
        cap_pack_kernel,
        [low(MESSAGE, QUARTER)] * 4,
        [SMEM] + [spec()] * 4 + [pl.BlockSpec(memory_space=pl.ANY)] * 4,
        [cap_rows] * 4,
        grid=(1,),
        moved=1000,
        name="cap_pack",
        aliases={5 + i: i for i in range(4)},
        scratch=[pltpu.VMEM((2 * CAP_PAD, WIDTH), F32)],
    )(scal, *caps, *packs)
    got = [packs[0]] + [lax.ppermute(packs[s], "seq", crossed(s)) for s in (1, 2, 3)]

    sent = call(
        temporal_pack_kernel,
        low(16, 4 * PIXELS, HALF),
        [spec()] * 2,
        spec(),
        moved=1000,
        name="temporal_pack",
        after=(packs[0],),
    )(temporal_qkv, out_grad)
    block = lax.all_to_all(
        sent, "seq", split_axis=0, concat_axis=0, tiled=True, axis_index_groups=GROUPS
    )

    message = spec((MESSAGE, HDIM), lambda h: (0, h))
    result = spec((5 * ROWS, HDIM), lambda h: (0, h))
    spatial = call(
        spatial_kernel,
        [low(5 * ROWS, QUARTER)] * 4,
        [SMEM] + [message] * 4,
        [result] * 4,
        grid=(3,),
        flops=100_000_000_000,
        moved=4_000_000,
        name="spatial_attention",
    )(scal, *got)

    caps = call(
        cap_join_kernel,
        low(80, HALF),
        [cap_rows] * 4,
        spec((80, HALF), lambda i: (0, 0)),
        grid=(1,),
        moved=300_000,
        name="cap_join",
        scratch=[pltpu.VMEM((80, HALF), F32)],
    )(*got)
    caps = [caps] + [lax.ppermute(caps, "seq", shifted(-s, 0)) for s in (1, 2, 3)]

    front = spec((2 * ROWS, HDIM), lambda h: (0, h))
    *done, c0, c1, c2, c3 = call(
        cross_kernel,
        [low(5 * ROWS, QUARTER)] * 4 + [low(2, 80, QUARTER)] * 4,
        [SMEM]
        + [spec((ROWS, HDIM), lambda h: (3, h))] * 4
        + [spec((ROWS, HDIM), lambda h: (4, h))] * 4
        + [spec((80, HDIM), lambda h: (0, h))] * 4
        + [spec((80, HDIM), lambda h: (0, h + 3))] * 4
        + [front] * 4,
        [front] * 4 + [spec((2, 80, HDIM), lambda h: (0, 0, h))] * 4,
        grid=(3,),
        flops=1_000_000_000,
        moved=3_000_000,
        name="cross_attention",
        aliases={17 + i: i for i in range(4)},
    )(scal, *got, *got, *caps, *caps, *spatial)
    back = [done[0]] + [lax.ppermute(done[s], "seq", crossed(s)) for s in (1, 2, 3)]
    block_spec = spec((FRAMES, 4 * PIXELS, HDIM), lambda h: (0, 0, h))
    solved = call(
        temporal_kernel,
        low(FRAMES, 4 * PIXELS, HALF),
        [SMEM, block_spec],
        block_spec,
        grid=(6,),
        flops=1_000_000,
        moved=10_000,
        name="temporal_attention",
        after=(back[1],),
    )(scal, block)
    returned = lax.all_to_all(
        solved, "seq", split_axis=0, concat_axis=0, tiled=True, axis_index_groups=GROUPS
    )
    sums = [c0] + [lax.ppermute(c, "seq", shifted(s, 0)) for s, c in ((1, c1), (2, c2), (3, c3))]
    both, spatial_grads, cross_query_grad = call(
        frame_unpack_kernel,
        [low(ROWS, WIDTH), low(3, ROWS, WIDTH), low(ROWS, WIDTH)],
        [SMEM] + [spec()] * 4,
        [spec()] * 3,
        flops=100_000_000_000,
        moved=4_000_000,
        name="frame_unpack",
        after=(solved,),
    )(scal, *back)

    sums = call(
        cap_sum_y_kernel,
        [low(CAP_SUMS, QUARTER)] * 4,
        [spec()] * 4,
        [spec()] * 4,
        moved=700_000,
        name="cap_sum_y",
        after=(both,),
        scratch=[pltpu.VMEM((2, 80, QUARTER), F32), pltpu.VMEM((CAP_SUMS, QUARTER), F32)],
    )(*sums)
    sums = [sums[0]] + [lax.ppermute(sums[s], "seq", shifted(0, s)) for s in (1, 2, 3)]
    sums = call(
        cap_sum_z_kernel,
        [full(2, 8, QUARTER)] * 4,
        [spec()] * 4,
        [spec()] * 4,
        moved=300_000,
        name="cap_sum_z",
        scratch=[pltpu.VMEM((CAP_SUMS, QUARTER), F32)],
    )(*sums)
    sums = [sums[0]] + [lax.ppermute(sums[s], "seq", crossed(s)) for s in (1, 2, 3)]
    steps = 4
    mixed, temporal_grads, token = call(
        temporal_unpack_kernel,
        [low(ROWS, WIDTH), low(3, ROWS, WIDTH), full(8, HDIM)],
        [
            SMEM,
            spec((16 // steps, 4 * PIXELS, HALF), lambda i: (i, 0, 0)),
            spec((ROWS // steps, WIDTH), lambda i: (i, 0)),
        ],
        [
            spec((ROWS // steps, WIDTH), lambda i: (i, 0)),
            spec((3, ROWS // steps, WIDTH), lambda i: (0, i, 0)),
            spec((8, HDIM), lambda i: (0, 0)),
        ],
        grid=(steps,),
        moved=3_600_000,
        name="temporal_unpack",
    )(scal, returned, both)

    sums = call(
        cap_place_kernel,
        full(2, 8, WIDTH),
        [SMEM] + [spec()] * 4,
        spec(),
        moved=200_000,
        name="cap_place",
        after=(token,),
    )(scal, *sums)
    caption_grads = jnp.swapaxes(sums[:, :5], 0, 1)
    return (mixed, spatial_grads, temporal_grads, cross_query_grad, caption_grads)


def solution(mesh):
    placed = (
        P(None, ("dp", "seq"), None),
        P(None, ("dp", "seq"), None),
        P(("dp", "seq"), None),
        P(("dp", "seq"), None, None),
        P(("dp", "seq"), None),
        P("dp"),
        P("dp"),
    )
    return jax.shard_map(
        local,
        mesh=mesh,
        in_specs=placed,
        out_specs=(
            P(("dp", "seq"), None),
            P(None, ("dp", "seq"), None),
            P(None, ("dp", "seq"), None),
            P(("dp", "seq"), None),
            P(("dp", "seq"), None, None),
        ),
        check_vma=False,
    )
```

```python
import functools

import jax
import jax.numpy as jnp
from jax import lax
from jax.experimental import pallas as pl
from jax.experimental.pallas import tpu as pltpu
from jax.sharding import PartitionSpec as P

HDIM = 128
ROWS = 128
WIDTH = 1536
FRAME_ROWS = 512
QUARTER = 384
HALF = 768
PIXELS = 16
FRAMES = 16
CAP_ROWS = 320
CAP_PAD = 32
CAP_SUMS = 48
MESSAGE = 5 * ROWS + 2 * CAP_PAD
SCALE = HDIM**-0.5
EXP2_SCALE = SCALE * 1.4426950408889634
BF16 = jnp.bfloat16
F32 = jnp.float32
VMEM_LIMIT = 48 * 2**20


def dot_nt(a, b):
    return lax.dot_general(a, b, (((1,), (1,)), ((), ())), preferred_element_type=F32)


def dot_tn(a, b):
    return lax.dot_general(a, b, (((0,), (0,)), ((), ())), preferred_element_type=F32)


def dot_nn(a, b):
    return lax.dot_general(a, b, (((1,), (0,)), ((), ())), preferred_element_type=F32)


def attend(q, k, v, g, keep=None):
    scores = dot_nt(k, q)
    if keep is not None:
        scores = jnp.where(keep, scores, -1e30)
    largest = jnp.max(scores, axis=0, keepdims=True)
    raised = jnp.exp2((scores - largest) * EXP2_SCALE)
    weights = raised * (1.0 / jnp.sum(raised, axis=0, keepdims=True))
    weights_low = weights.astype(BF16)
    dprobs = dot_nt(v, g)
    row_delta = jnp.sum(weights * dprobs, axis=0, keepdims=True)
    slopes = (weights * (dprobs - row_delta)).astype(BF16)
    out = dot_tn(weights_low, v)
    dq = dot_tn(slopes, k) * SCALE
    dk = dot_nn(slopes, q) * SCALE
    dv = dot_nn(weights_low, g)
    return out, dq, dk, dv


def frame_pack_kernel(scal, sqkv, grad, cq, *outs):
    for step, out in enumerate(outs):
        block = jnp.bitwise_xor(scal[0], step)
        lanes = pl.ds(pl.multiple_of(block * QUARTER, 128), QUARTER)
        for i in range(3):
            out[i * ROWS : (i + 1) * ROWS, :] = sqkv[i, :, lanes]
        out[3 * ROWS : 4 * ROWS, :] = grad[:, lanes]
        out[4 * ROWS : 5 * ROWS, :] = cq[:, lanes]


def temporal_pack_kernel(tqkv, grad, out):
    for group in range(8):
        rows = slice(group * PIXELS, (group + 1) * PIXELS)
        for half in range(2):
            lanes = slice(half * HALF, (half + 1) * HALF)
            for i in range(3):
                out[2 * group + half, i * PIXELS : (i + 1) * PIXELS, :] = tqkv[i, rows, lanes]
            out[2 * group + half, 3 * PIXELS : 4 * PIXELS, :] = grad[rows, lanes]


def live_grads(scal, parts):
    row = lax.broadcasted_iota(jnp.int32, (ROWS, HDIM), 0)
    grads = []
    for step, part in enumerate(parts):
        first = (scal[1] * 4 + jnp.bitwise_xor(scal[0], step)) * ROWS
        grads.append(jnp.where(row + first < scal[2], part.astype(F32), 0.0).astype(BF16))
    return jnp.concatenate(grads, axis=0)


def put_rows(outs, i, item):
    item = item.astype(BF16)
    for step, out in enumerate(outs):
        out[i * ROWS : (i + 1) * ROWS, :] = item[step * ROWS : (step + 1) * ROWS, :]


def spatial_kernel(scal, m0, m1, m2, m3, *outs):
    parts = (m0, m1, m2, m3)

    def joined(i):
        return jnp.concatenate([part[i * ROWS : (i + 1) * ROWS, :] for part in parts], axis=0)

    g = live_grads(scal, [part[3 * ROWS : 4 * ROWS, :] for part in parts])
    out, *grads = attend(joined(0), joined(1), joined(2), g)
    put_rows(outs, 0, out)
    for i, item in enumerate(grads):
        put_rows(outs, i + 2, item)


def cap_pack_kernel(scal, p0, p1, p2, p3, m0, m1, m2, m3, o0, o1, o2, o3, rows):
    rows[...] = jnp.zeros_like(rows)
    for i, part in enumerate((p0, p1, p2, p3)):
        for kind in range(2):
            first = kind * CAP_PAD + 5 * i
            rows[first : first + 5, :] = part[kind].astype(F32)
    for step, out in enumerate((o0, o1, o2, o3)):
        block = jnp.bitwise_xor(scal[0], step)
        lanes = pl.ds(pl.multiple_of(block * QUARTER, 128), QUARTER)
        out[...] = rows[:, lanes].astype(BF16)


def cap_join_kernel(m0, m1, m2, m3, out, rows):
    for i, part in enumerate((m0, m1, m2, m3)):
        for kind in range(2):
            item = part[kind * CAP_PAD : (kind + 1) * CAP_PAD, :].astype(F32)
            rows[20 * i : 20 * (i + 1), kind * QUARTER : (kind + 1) * QUARTER] = item[:20]
    out[...] = rows[...].astype(BF16)


def cap_sum_y_kernel(p0, p1, p2, p3, o0, o1, o2, o3, rows, picked):
    rows[...] = sum(part[...].astype(F32) for part in (p0, p1, p2, p3))
    picked[...] = jnp.zeros_like(picked)
    for z, out in enumerate((o0, o1, o2, o3)):
        for kind in range(2):
            for s in range(4):
                first, last = 20 * s + 5 * z, 20 * kind + 5 * s
                picked[last : last + 5, :] = rows[kind, first : first + 5, :]
        out[...] = picked[...].astype(BF16)


def cap_sum_z_kernel(p0, p1, p2, p3, o0, o1, o2, o3, rows):
    rows[...] = sum(part[...].astype(F32) for part in (p0, p1, p2, p3))
    for s, out in enumerate((o0, o1, o2, o3)):
        for kind in range(2):
            first = 20 * kind + 5 * s
            out[kind, :, :] = rows[first : first + 8, :]


def cap_place_kernel(scal, p0, p1, p2, p3, out):
    for step, part in enumerate((p0, p1, p2, p3)):
        block = jnp.bitwise_xor(scal[0], step)
        lanes = pl.ds(pl.multiple_of(block * QUARTER, 128), QUARTER)
        for kind in range(2):
            out[kind, :, lanes] = part[kind]


def cross_kernel(
    scal, g0, g1, g2, g3, q0, q1, q2, q3, c0, c1, c2, c3, d0, d1, d2, d3, s0, s1, s2, s3, *outs
):
    spatial = jnp.concatenate([s[0:ROWS, :] for s in (s0, s1, s2, s3)], axis=0)
    queries = jnp.concatenate([q0[...], q1[...], q2[...], q3[...]], axis=0)
    keys = jnp.concatenate([c0[...], c1[...], c2[...], c3[...]], axis=0)
    values = jnp.concatenate([d0[...], d1[...], d2[...], d3[...]], axis=0)
    g = live_grads(scal, [g0[...], g1[...], g2[...], g3[...]])
    slot = lax.broadcasted_iota(jnp.int32, (CAP_ROWS, 1), 0)
    five = jnp.right_shift(slot * 205, 10)
    owner_y = jnp.bitwise_and(jnp.right_shift(five, 4) + jnp.right_shift(scal[1], 2), 3)
    owner_z = jnp.bitwise_and(five + scal[1], 3)
    peer = jnp.bitwise_and(jnp.right_shift(five, 2), 3)
    owner = (owner_y * 4 + owner_z) * 4 + jnp.bitwise_xor(peer, scal[0])
    keep = owner * 5 + (slot - five * 5) < scal[3]
    out, dq, dk, dv = attend(queries, keys, values, g, keep)
    put_rows(outs[:4], 0, out + spatial.astype(F32))
    put_rows(outs[:4], 1, dq)
    for i in range(4):
        outs[4 + i][0, :, :] = dk[80 * i : 80 * (i + 1)].astype(BF16)
        outs[4 + i][1, :, :] = dv[80 * i : 80 * (i + 1)].astype(BF16)


def temporal_kernel(scal, block, out):
    size = FRAMES * PIXELS

    def rows_of(i):
        return block[:, i * PIXELS : (i + 1) * PIXELS, :].reshape(size, HDIM)

    first = scal[0] * ROWS + (scal[1] // 2) * PIXELS

    def token(shape, dim):
        place = lax.broadcasted_iota(jnp.int32, shape, dim)
        pixel = jnp.bitwise_and(place, PIXELS - 1)
        return pixel, (place // PIXELS) * FRAME_ROWS + first + pixel

    key_pixel, key_token = token((size, size), 0)
    query_pixel, _ = token((size, size), 1)
    keep = jnp.logical_and(key_pixel == query_pixel, key_token < scal[2])
    _, row_token = token((size, HDIM), 0)
    g = jnp.where(row_token < scal[2], rows_of(3).astype(F32), 0.0).astype(BF16)
    for i, item in enumerate(attend(rows_of(0), rows_of(1), rows_of(2), g, keep)):
        out[:, i * PIXELS : (i + 1) * PIXELS, :] = item.astype(BF16).reshape(FRAMES, PIXELS, HDIM)


def frame_unpack_kernel(scal, m0, m1, m2, m3, both, grads, cross_grad):
    for step, part in enumerate((m0, m1, m2, m3)):
        block = jnp.bitwise_xor(scal[0], step)
        lanes = pl.ds(pl.multiple_of(block * QUARTER, 128), QUARTER)
        both[:, lanes] = part[0:ROWS, :]
        cross_grad[:, lanes] = part[ROWS : 2 * ROWS, :]
        for i in range(3):
            grads[i, :, lanes] = part[(i + 2) * ROWS : (i + 3) * ROWS, :]


def temporal_unpack_kernel(scal, back, both, mixed, grads, token):
    token[...] = jnp.zeros_like(token)
    first = (scal[1] * 4 + scal[0]) * ROWS + pl.program_id(0) * PIXELS * (back.shape[0] // 2)
    row = lax.broadcasted_iota(jnp.int32, (PIXELS, HALF), 0)
    for group in range(back.shape[0] // 2):
        rows = slice(group * PIXELS, (group + 1) * PIXELS)
        live = row + (first + group * PIXELS) < scal[2]
        for half in range(2):
            lanes = slice(half * HALF, (half + 1) * HALF)
            t = 2 * group + half
            total = back[t, 0:PIXELS, :].astype(F32) + both[rows, lanes].astype(F32)
            mixed[rows, lanes] = jnp.where(live, total, 0.0).astype(BF16)
            for i in range(3):
                grads[i, rows, lanes] = back[t, (i + 1) * PIXELS : (i + 2) * PIXELS, :]


def spec(shape=None, index=None):
    if shape is None:
        return pl.BlockSpec(memory_space=pltpu.VMEM)
    return pl.BlockSpec(shape, index)


SMEM = pl.BlockSpec(memory_space=pltpu.SMEM)


def call(
    kernel,
    out_shape,
    in_specs,
    out_specs,
    grid=None,
    flops=0,
    moved=0,
    name=None,
    after=(),
    scratch=(),
    aliases=None,
):
    options = {} if grid is None else {"grid": grid}
    known = len(in_specs)

    def body(*refs):
        kernel(*refs[:known], *refs[known + len(after) :])

    made = pl.pallas_call(
        body,
        out_shape=out_shape,
        in_specs=list(in_specs) + [pl.BlockSpec(memory_space=pl.ANY)] * len(after),
        out_specs=out_specs,
        scratch_shapes=list(scratch),
        input_output_aliases=aliases or {},
        compiler_params=pltpu.CompilerParams(vmem_limit_bytes=VMEM_LIMIT),
        cost_estimate=pl.CostEstimate(flops=flops, bytes_accessed=moved, transcendentals=0),
        name=name,
        **options,
    )
    return lambda *args: made(*args, *after)


def low(*shape):
    return jax.ShapeDtypeStruct(shape, BF16)


def full(*shape):
    return jax.ShapeDtypeStruct(shape, F32)


def place(y, z, r):
    return (y % 4) * 16 + (z % 4) * 4 + r


def shifted(dy, dz):
    return [
        (place(y, z, r), place(y + dy, z + dz, r))
        for y in range(4)
        for z in range(4)
        for r in range(4)
    ]


def crossed(step):
    return [(i, i ^ step) for i in range(64)]


GROUPS = [[4 * f + r for f in range(16)] for r in range(4)]


def local(spatial_qkv, temporal_qkv, cross_query, caption_kv, out_grad, live_tokens, caption_len):
    index = lax.axis_index("seq").astype(jnp.int32)
    me, frame = index % 4, index // 4
    scal = jnp.stack([me, frame, live_tokens[0], caption_len[0]])

    packs = call(
        frame_pack_kernel,
        [low(MESSAGE, QUARTER)] * 4,
        [SMEM] + [spec()] * 3,
        [spec((5 * ROWS, QUARTER), lambda i: (0, 0))] * 4,
        grid=(1,),
        moved=1000,
        name="frame_pack",
    )(scal, spatial_qkv, out_grad, cross_query)
    caps = jnp.swapaxes(caption_kv, 0, 1)
    caps = [caps] + [lax.ppermute(caps, "seq", shifted(0, -s)) for s in (1, 2, 3)]
    cap_rows = spec((2 * CAP_PAD, QUARTER), lambda i: (5 * ROWS // (2 * CAP_PAD), 0))
    packs = call(
        cap_pack_kernel,
        [low(MESSAGE, QUARTER)] * 4,
        [SMEM] + [spec()] * 4 + [pl.BlockSpec(memory_space=pl.ANY)] * 4,
        [cap_rows] * 4,
        grid=(1,),
        moved=1000,
        name="cap_pack",
        aliases={5 + i: i for i in range(4)},
        scratch=[pltpu.VMEM((2 * CAP_PAD, WIDTH), F32)],
    )(scal, *caps, *packs)
    got = [packs[0]] + [lax.ppermute(packs[s], "seq", crossed(s)) for s in (1, 2, 3)]

    sent = call(
        temporal_pack_kernel,
        low(16, 4 * PIXELS, HALF),
        [spec()] * 2,
        spec(),
        moved=1000,
        name="temporal_pack",
        after=(packs[0],),
    )(temporal_qkv, out_grad)
    block = lax.all_to_all(
        sent, "seq", split_axis=0, concat_axis=0, tiled=True, axis_index_groups=GROUPS
    )

    message = spec((MESSAGE, HDIM), lambda h: (0, h))
    result = spec((5 * ROWS, HDIM), lambda h: (0, h))
    spatial = call(
        spatial_kernel,
        [low(5 * ROWS, QUARTER)] * 4,
        [SMEM] + [message] * 4,
        [result] * 4,
        grid=(3,),
        flops=100_000_000_000,
        moved=4_000_000,
        name="spatial_attention",
    )(scal, *got)

    caps = call(
        cap_join_kernel,
        low(80, HALF),
        [cap_rows] * 4,
        spec((80, HALF), lambda i: (0, 0)),
        grid=(1,),
        moved=300_000,
        name="cap_join",
        scratch=[pltpu.VMEM((80, HALF), F32)],
    )(*got)
    caps = [caps] + [lax.ppermute(caps, "seq", shifted(-s, 0)) for s in (1, 2, 3)]

    front = spec((2 * ROWS, HDIM), lambda h: (0, h))
    *done, c0, c1, c2, c3 = call(
        cross_kernel,
        [low(5 * ROWS, QUARTER)] * 4 + [low(2, 80, QUARTER)] * 4,
        [SMEM]
        + [spec((ROWS, HDIM), lambda h: (3, h))] * 4
        + [spec((ROWS, HDIM), lambda h: (4, h))] * 4
        + [spec((80, HDIM), lambda h: (0, h))] * 4
        + [spec((80, HDIM), lambda h: (0, h + 3))] * 4
        + [front] * 4,
        [front] * 4 + [spec((2, 80, HDIM), lambda h: (0, 0, h))] * 4,
        grid=(3,),
        flops=1_000_000_000,
        moved=3_000_000,
        name="cross_attention",
        aliases={17 + i: i for i in range(4)},
    )(scal, *got, *got, *caps, *caps, *spatial)
    back = [done[0]] + [lax.ppermute(done[s], "seq", crossed(s)) for s in (1, 2, 3)]
    block_spec = spec((FRAMES, 4 * PIXELS, HDIM), lambda h: (0, 0, h))
    solved = call(
        temporal_kernel,
        low(FRAMES, 4 * PIXELS, HALF),
        [SMEM, block_spec],
        block_spec,
        grid=(6,),
        flops=1_000_000,
        moved=10_000,
        name="temporal_attention",
        after=(back[1],),
    )(scal, block)
    returned = lax.all_to_all(
        solved, "seq", split_axis=0, concat_axis=0, tiled=True, axis_index_groups=GROUPS
    )
    sums = [c0] + [lax.ppermute(c, "seq", shifted(s, 0)) for s, c in ((1, c1), (2, c2), (3, c3))]
    both, spatial_grads, cross_query_grad = call(
        frame_unpack_kernel,
        [low(ROWS, WIDTH), low(3, ROWS, WIDTH), low(ROWS, WIDTH)],
        [SMEM] + [spec()] * 4,
        [spec()] * 3,
        flops=100_000_000_000,
        moved=4_000_000,
        name="frame_unpack",
        after=(solved,),
    )(scal, *back)

    sums = call(
        cap_sum_y_kernel,
        [low(CAP_SUMS, QUARTER)] * 4,
        [spec()] * 4,
        [spec()] * 4,
        moved=700_000,
        name="cap_sum_y",
        after=(both,),
        scratch=[pltpu.VMEM((2, 80, QUARTER), F32), pltpu.VMEM((CAP_SUMS, QUARTER), F32)],
    )(*sums)
    sums = [sums[0]] + [lax.ppermute(sums[s], "seq", shifted(0, s)) for s in (1, 2, 3)]
    sums = call(
        cap_sum_z_kernel,
        [full(2, 8, QUARTER)] * 4,
        [spec()] * 4,
        [spec()] * 4,
        moved=300_000,
        name="cap_sum_z",
        scratch=[pltpu.VMEM((CAP_SUMS, QUARTER), F32)],
    )(*sums)
    sums = [sums[0]] + [lax.ppermute(sums[s], "seq", crossed(s)) for s in (1, 2, 3)]
    steps = 2
    mixed, temporal_grads, token = call(
        temporal_unpack_kernel,
        [low(ROWS, WIDTH), low(3, ROWS, WIDTH), full(8, HDIM)],
        [
            SMEM,
            spec((16 // steps, 4 * PIXELS, HALF), lambda i: (i, 0, 0)),
            spec((ROWS // steps, WIDTH), lambda i: (i, 0)),
        ],
        [
            spec((ROWS // steps, WIDTH), lambda i: (i, 0)),
            spec((3, ROWS // steps, WIDTH), lambda i: (0, i, 0)),
            spec((8, HDIM), lambda i: (0, 0)),
        ],
        grid=(steps,),
        moved=3_600_000,
        name="temporal_unpack",
    )(scal, returned, both)

    sums = call(
        cap_place_kernel,
        full(2, 8, WIDTH),
        [SMEM] + [spec()] * 4,
        spec(),
        moved=200_000,
        name="cap_place",
        after=(token,),
    )(scal, *sums)
    caption_grads = jnp.swapaxes(sums[:, :5], 0, 1)
    return (mixed, spatial_grads, temporal_grads, cross_query_grad, caption_grads)


def solution(mesh):
    placed = (
        P(None, ("dp", "seq"), None),
        P(None, ("dp", "seq"), None),
        P(("dp", "seq"), None),
        P(("dp", "seq"), None, None),
        P(("dp", "seq"), None),
        P("dp"),
        P("dp"),
    )
    return jax.shard_map(
        local,
        mesh=mesh,
        in_specs=placed,
        out_specs=(
            P(("dp", "seq"), None),
            P(None, ("dp", "seq"), None),
            P(None, ("dp", "seq"), None),
            P(("dp", "seq"), None),
            P(("dp", "seq"), None, None),
        ),
        check_vma=False,
    )
```
